512 devices in a mesh: seq: 32 (over x, z), tp: 16 (over y, core).
Axes of the slice: x: 4, y: 8, z: 8, core: 2. Of those that a mesh axis runs over, the one named last changes fastest.
Arguments:
- tokens: bfloat16 [32, 192, 3072], P('seq', None, 'tp'), may hold values from -17 to 17
- spatial_query: bfloat16 [32, 192, 2048], P('seq', None, 'tp'), may hold values from -4 to 4
- spatial_key: bfloat16 [32, 192, 2048], P('seq', None, 'tp'), may hold values from -4 to 4
- spatial_value: bfloat16 [32, 192, 2048], P('seq', None, 'tp'), may hold values from -5 to 5
- spatial_gain: float32 [2, 16, 128], P(None, 'tp'), may hold values from 0.5 to 4.5
- spatial_proj: bfloat16 [2048, 3072], P('tp'), may hold values from -0.5 to 0.5
- spatial_gate: float32 [3072], replicated, may hold values from -3 to 3
- temporal_shift: float32 [3072], replicated, may hold values from -2.5 to 2.5
- temporal_scale: float32 [3072], replicated, may hold values from -2.5 to 2.5
- temporal_weights: bfloat16 [3072, 16, 3, 128], P(None, 'tp'), may hold values from -0.073973 to 0.073973
- temporal_gain: float32 [2, 16, 128], P(None, 'tp'), may hold values from 0.5 to 4.5
- temporal_proj: bfloat16 [2048, 3072], P('tp'), may hold values from -0.5 to 0.5
- temporal_gate: float32 [3072], replicated, may hold values from -3 to 3
Outputs:
- block_output: bfloat16 [32, 192, 3072], P(None, 'seq', 'tp')
The draws below stay inside these ranges and needn't reach their ends.
All inputs are finite; a program needn't handle non-finite values.
Results may differ from the reference program's by a relative error of at most 0.029.
Values may be sent and summed in bfloat16 or wider, within the bound.
A program may use at most 64 MiB of HBM per device.

```python
import math
import jax
import jax.numpy as jnp
from jax import lax

D = 3072
HEADS = 16
HD = 128
FRAMES = 32
SPACE = 192
N_TP = 16


def spatial_pair(key):
    key_first = jax.random.fold_in(key, 0)
    key_third = jax.random.fold_in(key, 2)
    shape = (FRAMES, SPACE, HEADS * HD)
    key_rows = jnp.clip(jax.random.normal(key_first, shape, jnp.float32), -4.0, 4.0)
    query_rows = jnp.clip(jax.random.normal(key_third, shape, jnp.float32), -4.0, 4.0)
    return (query_rows, key_rows)


def gain_table(key):
    key_first = jax.random.fold_in(key, 0)
    return jnp.exp(jax.random.uniform(key_first, (2, HEADS, HD), jnp.float32, math.log(0.6), math.log(1.6)))


def draw_spatial_query(key, part):
    pair = spatial_pair(key)
    return pair[0].astype(jnp.bfloat16)


def draw_spatial_key(key, part):
    pair = spatial_pair(key)
    return pair[1].astype(jnp.bfloat16)


def draw_tokens(key, part):
    key = jax.random.fold_in(key, 3)
    key_first = jax.random.fold_in(key, 0)
    shape = (FRAMES, SPACE, D)
    values = jnp.clip(jax.random.normal(key_first, shape, jnp.float32), -4.0, 4.0)
    return values.astype(jnp.bfloat16)


def draw_temporal_weights(key, part):
    key = jax.random.fold_in(key, 4)
    key_first, key_second, key_third = jax.random.split(key, 3)
    shape = (D, HEADS, 1, HD)
    factor = D ** (-0.5)
    query_part = jnp.clip(jax.random.normal(key_first, shape, jnp.float32), -4.0, 4.0)
    key_part = jnp.clip(jax.random.normal(key_second, shape, jnp.float32), -4.0, 4.0)
    value_part = jnp.clip(jax.random.normal(key_third, shape, jnp.float32), -4.0, 4.0)
    stacked = jnp.concatenate([query_part, key_part, value_part], axis=2) * factor
    return stacked.astype(jnp.bfloat16)


def draw_spatial_gain(key, part):
    key = jax.random.fold_in(key, 5)
    return gain_table(key)


def draw_temporal_gain(key, part):
    key = jax.random.fold_in(key, 6)
    return gain_table(key)


def block_levels(rng, shape, cuts, least, top_value):
    def one(position, parts):
        heights = jax.random.uniform(jax.random.fold_in(jax.random.fold_in(rng, 6), position), (parts,), jnp.float32, least / len(cuts), top_value / len(cuts))
        return jnp.repeat(jnp.exp(heights), shape[position] // parts).reshape((-1,) + (1,) * (len(shape) - position - 1))

    loudness = one(*cuts[0])
    for cut in cuts[1:]:
        loudness = loudness * one(*cut)
    return loudness


def gaussian(rng, shape, scale, most, pieces=(), dtype=jnp.bfloat16):
    result = scale * jax.random.normal(rng, shape, jnp.float32)
    if pieces:
        result = result * block_levels(rng, shape, pieces, -0.22, 0.18)
    return jnp.clip(result, -most, most).astype(dtype)


def setup_inputs(seed: int = 0) -> dict:
    splits = jax.random.split(jax.random.key(seed), 14)
    return {
        "tokens": draw_tokens(jax.random.fold_in(splits[13], 71), 0),
        "spatial_query": draw_spatial_query(jax.random.fold_in(splits[13], 71), 0),
        "spatial_key": draw_spatial_key(jax.random.fold_in(splits[13], 71), 0),
        "spatial_value": gaussian(splits[3], (FRAMES, SPACE, HEADS * HD), 1.0, 5.0, ((0, 32), (2, 16))),
        "spatial_gain": draw_spatial_gain(jax.random.fold_in(splits[13], 71), 0),
        "spatial_proj": gaussian(splits[5], (HEADS * HD, D), HD ** -0.5, 0.5, ((0, 16),)),
        "spatial_gate": gaussian(splits[6], (D,), 1.0, 3.0, (), jnp.float32),
        "temporal_shift": gaussian(splits[7], (D,), 0.5, 2.5, (), jnp.float32),
        "temporal_scale": gaussian(splits[8], (D,), 0.5, 2.5, (), jnp.float32),
        "temporal_weights": draw_temporal_weights(jax.random.fold_in(splits[13], 71), 0),
        "temporal_gain": draw_temporal_gain(jax.random.fold_in(splits[13], 71), 0),
        "temporal_proj": gaussian(splits[11], (HEADS * HD, D), HD ** -0.5, 0.5, ((0, 16),)),
        "temporal_gate": gaussian(splits[12], (D,), 1.0, 3.0, (), jnp.float32),
    }


NORM_EPS = 1e-06

def head_norm(values, gain):
    square_mean = lax.optimization_barrier(jnp.mean(values * values, axis=-1, keepdims=True))
    return (values * lax.rsqrt(square_mean + NORM_EPS) * gain).astype(jnp.bfloat16)

def modulated_norm(rows, scale_vec, shift_vec):
    centre = rows - lax.optimization_barrier(jnp.mean(rows, axis=-1, keepdims=True))
    variance = lax.optimization_barrier(jnp.mean(centre * centre, axis=-1, keepdims=True))
    return (centre * lax.rsqrt(variance + NORM_EPS) * (1.0 + scale_vec) + shift_vec).astype(jnp.bfloat16)

def group_sum(rows, weight):
    inner = HEADS * HD
    group_width = inner // N_TP
    grouped = rows.reshape(rows.shape[0], N_TP, group_width).transpose(1, 0, 2)
    weight_groups = weight.reshape(N_TP, group_width, D)

    def add_group(total, pair):
        product = jnp.dot(pair[0], pair[1], preferred_element_type=jnp.float32)
        rounded = lax.optimization_barrier(product.astype(jnp.bfloat16))
        return (total + rounded.astype(jnp.float32), None)
    start_total = jnp.zeros((rows.shape[0], D), jnp.float32)
    total, unused = lax.scan(add_group, start_total, (grouped, weight_groups))
    return total

def reference(tokens, spatial_query, spatial_key, spatial_value, spatial_gain, spatial_proj, spatial_gate, temporal_shift, temporal_scale, temporal_weights, temporal_gain, temporal_proj, temporal_gate):
    inner = HEADS * HD
    score_scale = HD ** (-0.5)

    def spatial_frame(triple):
        query_rows = head_norm(triple[0].astype(jnp.float32).reshape(SPACE, HEADS, HD), spatial_gain[0])
        key_rows = head_norm(triple[1].astype(jnp.float32).reshape(SPACE, HEADS, HD), spatial_gain[1])
        scores = jnp.einsum('shd,thd->hst', query_rows.astype(jnp.float32), key_rows.astype(jnp.float32)) * score_scale
        attention = jax.nn.softmax(scores, axis=-1).astype(jnp.bfloat16)
        value_rows = triple[2].reshape(SPACE, HEADS, HD)
        heads_out = jnp.einsum('hst,thd->shd', attention.astype(jnp.float32), value_rows.astype(jnp.float32))
        return heads_out.astype(jnp.bfloat16).reshape(SPACE, inner)
    spatial_heads = lax.map(spatial_frame, (spatial_query, spatial_key, spatial_value))
    proj_first = group_sum(spatial_heads.reshape(FRAMES * SPACE, inner), spatial_proj)
    mid_tokens = (tokens.astype(jnp.float32) + spatial_gate * proj_first.reshape(FRAMES, SPACE, D)).astype(jnp.bfloat16)
    modulated = modulated_norm(mid_tokens.astype(jnp.float32), temporal_scale, temporal_shift)
    projected = jnp.dot(modulated.reshape(FRAMES * SPACE, D), temporal_weights.reshape(D, 3 * inner), preferred_element_type=jnp.float32).reshape(FRAMES, SPACE, HEADS, 3, HD)
    query_time = head_norm(projected[:, :, :, 0, :], temporal_gain[0])
    key_time = head_norm(projected[:, :, :, 1, :], temporal_gain[1])
    value_time = projected[:, :, :, 2, :].astype(jnp.bfloat16)
    scores_time = jnp.einsum('fshd,gshd->shfg', query_time.astype(jnp.float32), key_time.astype(jnp.float32)) * score_scale
    attention_time = jax.nn.softmax(scores_time, axis=-1).astype(jnp.bfloat16)
    temporal_heads = jnp.einsum('shfg,gshd->fshd', attention_time.astype(jnp.float32), value_time.astype(jnp.float32))
    temporal_heads = temporal_heads.astype(jnp.bfloat16).reshape(FRAMES * SPACE, inner)
    proj_second = group_sum(temporal_heads, temporal_proj)
    block_output = mid_tokens.astype(jnp.float32) + temporal_gate * proj_second.reshape(FRAMES, SPACE, D)
    return block_output.astype(jnp.bfloat16)
```

```python
import functools

import jax
import jax.numpy as jnp
from jax import lax
from jax.experimental import pallas as pl
from jax.experimental.pallas import tpu as pltpu
from jax.sharding import PartitionSpec as P

NORM_EPS = 1e-06
MESH = pl.DeviceIdType.MESH
BF16 = jnp.bfloat16
F32 = jnp.float32

NX, NZ, NY = 4, 8, 8
NSEQ = NX * NZ
FRAMES = 32
SPACE = 192
PLACES = SPACE // NSEQ
HALF = PLACES // 2
HD = 128
D = 3072
ROWS = HALF * FRAMES
FEAT = D // NY
SLICE = FEAT // 2
SLAB = 16
SCALE = HD**-0.5


def head_norm(values, gain):
    square_mean = jnp.mean(values * values, axis=-1, keepdims=True)
    return (values * lax.rsqrt(square_mean + NORM_EPS) * gain).astype(BF16)


def dot(a, b):
    return jnp.dot(a, b, preferred_element_type=F32)


def dot_t(a, b):
    return lax.dot_general(a, b, (((1,), (1,)), ((), ())), preferred_element_type=F32)


def one_hot(targets, columns):
    rows = targets.shape[0]
    return jnp.where(
        lax.broadcasted_iota(jnp.int32, (rows, columns), 1) == targets, 1.0, 0.0
    ).astype(BF16)


def row_iota(rows):
    return lax.broadcasted_iota(jnp.int32, (rows, 1), 0)


def kernel(
    tok_h, q_h, k_h, v_h, sgain_h, proj_h, sgate_h, shift_h, scale_h, w_h, tgain_h, proj2_h, tgate_h,
    out_ref,
    tok, q, k, v, sgain, proj, sgate, shift, scale, w, tgain, proj2, tgate,
    heads, slab_out, slab_in, pick, hv, hs, tokbuf, toksend, part_out, part_in, mid, th,
    part2_out, part2_in, osend, orecv,
    load_sem, wsend, wrecv, a_send, a_recv, x_send, x_recv, e1s, e1r, e2s, e2r, e3s, e3r,
):
    s = lax.axis_index("seq")
    t = lax.axis_index("tp")
    y = t // 2
    c = t % 2
    xx = s // NZ
    z = s % NZ
    sib = (s, t + 1 - 2 * c)

    def ydev(step):
        return (s, 2 * ((y + step) % NY) + c)

    def seq_peer(dx, dz):
        return ((xx + dx) % NX) * NZ + (z + dz) % NZ

    hops = sorted(
        [(dx, dz) for dx in range(NX) for dz in range(NZ) if dx or dz],
        key=lambda d: -(min(d[0], NX - d[0]) + min(d[1], NZ - d[1])),
    )

    def remote(src, dst, ss, rs, device):
        return pltpu.make_async_remote_copy(
            src_ref=src, dst_ref=dst, send_sem=ss, recv_sem=rs, device_id=device, device_id_type=MESH
        )

    own_cols = pl.multiple_of(c * (3 * HD), HD)
    rows_c = pl.multiple_of(c * HD, HD)
    loads = [
        (q_h.at[0], q), (k_h.at[0], k), (v_h.at[0], v), (sgain_h, sgain), (tok_h.at[0], tok),
        (proj_h, proj.at[pl.ds(rows_c, HD)]), (sgate_h, sgate),
        (scale_h, scale), (shift_h, shift), (tgain_h, tgain.at[c]),
        (w_h.at[0], w.at[:, pl.ds(own_cols, HD)]),
        (w_h.at[1], w.at[:, pl.ds(pl.multiple_of(own_cols + HD, HD), HD)]),
        (w_h.at[2], w.at[:, pl.ds(pl.multiple_of(own_cols + 2 * HD, HD), HD)]),
        (proj2_h, proj2.at[pl.ds(rows_c, HD)]), (tgate_h, tgate),
    ]
    loads = [pltpu.make_async_copy(a, b, load_sem.at[i]) for i, (a, b) in enumerate(loads)]
    for copy in loads:
        copy.start()

    barrier = pltpu.get_barrier_semaphore()
    for dx, dz in hops:
        pl.semaphore_signal(barrier, inc=1, device_id=(seq_peer(dx, dz), t), device_id_type=MESH)
    for step in range(1, NY):
        pl.semaphore_signal(barrier, inc=1, device_id=ydev(step), device_id_type=MESH)
    pl.semaphore_signal(barrier, inc=1, device_id=sib, device_id_type=MESH)

    for copy in loads[:4]:
        copy.wait()
    qn = head_norm(q[...].astype(F32), sgain[0])
    kn = head_norm(k[...].astype(F32), sgain[1])
    sc = dot_t(qn, kn) * SCALE
    ex = jnp.exp(sc - jnp.max(sc, axis=-1, keepdims=True))
    at = (ex / jnp.sum(ex, axis=-1, keepdims=True)).astype(BF16)
    heads[...] = dot(at, v[...]).astype(BF16)

    r = row_iota(NSEQ * SLAB)
    j, i = r // SLAB, r % SLAB
    loads[4].wait()
    tk = tok[...]
    col = lax.broadcasted_iota(jnp.int32, (SLICE, 2 * HD), 1)
    row = lax.broadcasted_iota(jnp.int32, (SLICE, 2 * HD), 0)
    rest = SLICE - HD
    spread = jnp.where(
        (row >= HD) & ((col == row - HD) | (col == row - HD + HD + rest)), 1.0, 0.0
    ).astype(BF16)
    tail = dot(tk, spread).astype(BF16)
    slab = dot(one_hot(jnp.where(i < PLACES, PLACES * j + i, -1), SPACE), heads[...])
    slab += dot(
        one_hot(jnp.where((i >= PLACES) & (i < 2 * PLACES), PLACES * j + i - PLACES, -1), SPACE), tk[:, :HD]
    )
    last = (i >= 2 * PLACES) & (i < 2 * PLACES + HALF)
    slab += dot(one_hot(jnp.where(last, PLACES * j + i - 2 * PLACES, -1), SPACE), tail[:, :HD])
    slab += dot(one_hot(jnp.where(last, PLACES * j + HALF + i - 2 * PLACES, -1), SPACE), tail[:, HD:])
    slab_out[...] = slab.astype(BF16).reshape(NSEQ, SLAB, HD)

    pl.semaphore_wait(barrier, len(hops) + NY)

    switch = [
        remote(slab_out.at[seq_peer(dx, dz)], slab_in.at[s], a_send.at[n], a_recv.at[n], (seq_peer(dx, dz), t))
        for n, (dx, dz) in enumerate(hops)
    ]
    for copy in switch:
        copy.start()
    slab_in[s] = slab_out[s]

    weights = [
        (proj_h, proj.at[pl.ds(rows_c, HD)]), (tgain_h, tgain.at[c]),
        (w_h.at[0], w.at[:, pl.ds(own_cols, HD)]),
        (w_h.at[1], w.at[:, pl.ds(pl.multiple_of(own_cols + HD, HD), HD)]),
        (w_h.at[2], w.at[:, pl.ds(pl.multiple_of(own_cols + 2 * HD, HD), HD)]),
        (proj2_h, proj2.at[pl.ds(rows_c, HD)]),
    ]
    weights = [remote(a, b, wsend.at[n], wrecv.at[n], sib) for n, (a, b) in enumerate(weights)]
    for copy in weights:
        copy.start()

    r = row_iota(ROWS)
    p, f = r // FRAMES, r % FRAMES
    pick[0] = one_hot(SLAB * f + HALF * c + p, NSEQ * SLAB)
    pick[1] = one_hot(SLAB * f + HALF * (1 - c) + p, NSEQ * SLAB)
    pick[2] = one_hot(SLAB * f + PLACES + HALF * c + p, NSEQ * SLAB)
    pick[3] = one_hot(SLAB * f + PLACES + HALF * (1 - c) + p, NSEQ * SLAB)
    pick[4] = one_hot(SLAB * f + 2 * PLACES + p, NSEQ * SLAB)

    for copy in switch:
        copy.wait_recv()
    got = slab_in[...].reshape(NSEQ * SLAB, HD)
    hs[...] = dot(pick[1], got).astype(BF16)
    swap_heads = remote(hs, hv.at[c], x_send.at[0], x_recv.at[0], sib)
    swap_heads.start()
    hv[c] = dot(pick[0], got).astype(BF16)
    toksend[:, :HD] = dot(pick[3], got).astype(BF16)
    third = dot(pick[4], got).astype(BF16)
    toksend[:, HD:] = third
    swap_tok = remote(toksend, tokbuf.at[c], x_send.at[1], x_recv.at[1], sib)
    swap_tok.start()
    tokbuf[c, :, :HD] = dot(pick[2], got).astype(BF16)
    tokbuf[c, :, HD:] = third

    def exchange(rows_a, rows_b, weight, buf_out, buf_in, ss, rs):
        copies = []
        for step in (4, 3, 5, 2, 6, 1, 7):
            cols = pl.ds(pl.multiple_of(((y + step) % NY) * FEAT, HD), FEAT)
            buf_out[step] = (dot(rows_a, weight[:HD, cols]) + dot(rows_b, weight[HD:, cols])).astype(BF16)
            copy = remote(buf_out.at[step], buf_in.at[step], ss.at[step], rs.at[step], ydev(step))
            copy.start()
            copies.append((step, copy))
        cols = pl.ds(pl.multiple_of(y * FEAT, HD), FEAT)
        return dot(rows_a, weight[:HD, cols]) + dot(rows_b, weight[HD:, cols]), copies

    def total_of(total, copies, buf_in):
        for step, copy in reversed(copies):
            copy.wait_recv()
            total = total + buf_in[step].astype(F32)
        return total

    loads[5].wait()
    weights[0].wait_recv()
    swap_heads.wait_recv()
    total, first = exchange(hv[0], hv[1], proj, part_out, part_in, e1s, e1r)

    swap_tok.wait_recv()
    lane = lax.broadcasted_iota(jnp.int32, (2 * HD, 1), 0)
    inner = lane - HD - rest * c
    base = jnp.where(lane < HD, lane, jnp.where((inner >= 0) & (inner < rest), HD + inner, -FEAT))
    own_tok = dot(tokbuf[0], one_hot(base, FEAT)) + dot(tokbuf[1], one_hot(base + SLICE, FEAT))

    loads[6].wait()
    cols_y = pl.ds(pl.multiple_of(y * FEAT, HD), FEAT)
    total = total_of(total, first, part_in)
    mid[y] = (own_tok + sgate[:, cols_y] * total).astype(BF16)

    gathers = []
    for step in (4, 3, 5, 2, 6, 1, 7):
        copy = remote(mid.at[y], mid.at[y], e2s.at[step], e2r.at[step], ydev(step))
        copy.start()
        gathers.append(copy)
    for copy in loads[7:]:
        copy.wait()
    for copy in weights[1:]:
        copy.wait_recv()
    for copy in gathers:
        copy.wait_recv()

    sums = jnp.zeros((ROWS, 1), F32)
    for n in range(NY):
        sums += jnp.sum(mid[n].astype(F32), axis=-1, keepdims=True)
    mean = sums * (1.0 / D)
    squares = jnp.zeros((ROWS, 1), F32)
    for n in range(NY):
        centre = mid[n].astype(F32) - mean
        squares += jnp.sum(centre * centre, axis=-1, keepdims=True)
    inv = lax.rsqrt(squares * (1.0 / D) + NORM_EPS)
    acc = jnp.zeros((ROWS, 6 * HD), F32)
    for n in range(NY):
        cols = slice(n * FEAT, (n + 1) * FEAT)
        modulated = ((mid[n].astype(F32) - mean) * inv * (1.0 + scale[:, cols]) + shift[:, cols]).astype(BF16)
        acc += dot(modulated, w[cols, :])

    same = (lax.broadcasted_iota(jnp.int32, (ROWS, ROWS), 0) // FRAMES) == (
        lax.broadcasted_iota(jnp.int32, (ROWS, ROWS), 1) // FRAMES
    )
    for n in range(2):
        part = acc[:, 3 * HD * n : 3 * HD * (n + 1)]
        qt = head_norm(part[:, :HD], tgain[n, 0])
        kt = head_norm(part[:, HD : 2 * HD], tgain[n, 1])
        vt = part[:, 2 * HD :].astype(BF16)
        st = jnp.where(same, dot_t(qt, kt) * SCALE, -1e30)
        et = jnp.where(same, jnp.exp(st - jnp.max(st, axis=-1, keepdims=True)), 0.0)
        att = (et / jnp.sum(et, axis=-1, keepdims=True)).astype(BF16)
        th[n] = dot(att, vt).astype(BF16)

    total, second = exchange(th[0], th[1], proj2, part2_out, part2_in, e3s, e3r)
    total = total_of(total, second, part2_in)
    out = (mid[y].astype(F32) + tgate[:, cols_y] * total).astype(BF16)

    feature = lax.broadcasted_iota(jnp.int32, (FEAT, SLICE), 0)
    column = lax.broadcasted_iota(jnp.int32, (FEAT, SLICE), 1)
    give = jnp.where(feature == column + SLICE * (1 - c), 1.0, 0.0).astype(BF16)
    keep = jnp.where(feature == column + SLICE * c, 1.0, 0.0).astype(BF16)
    osend[...] = dot(out, give).astype(BF16)
    swap_out = remote(osend, orecv, x_send.at[2], x_recv.at[2], sib)
    swap_out.start()
    out_ref[pl.ds(HALF * c, HALF)] = dot(out, keep).astype(BF16).reshape(HALF, FRAMES, SLICE)
    swap_out.wait_recv()
    out_ref[pl.ds(HALF * (1 - c), HALF)] = orecv[...].reshape(HALF, FRAMES, SLICE)

    for copy in switch + weights + gathers + [swap_heads, swap_tok, swap_out]:
        copy.wait_send()
    for step, copy in first + second:
        copy.wait_send()


def local(
    tokens, spatial_query, spatial_key, spatial_value, spatial_gain, spatial_proj, spatial_gate,
    temporal_shift, temporal_scale, temporal_weights, temporal_gain, temporal_proj, temporal_gate,
):
    vm = pltpu.VMEM
    dma = pltpu.SemaphoreType.DMA
    any_spec = pl.BlockSpec(memory_space=pltpu.HBM)
    out = pl.pallas_call(
        kernel,
        out_shape=jax.ShapeDtypeStruct((PLACES, FRAMES, SLICE), BF16),
        in_specs=[any_spec] * 13,
        out_specs=pl.BlockSpec(memory_space=pltpu.VMEM),
        scratch_shapes=[
            vm((SPACE, SLICE), BF16), vm((SPACE, HD), BF16), vm((SPACE, HD), BF16), vm((SPACE, HD), BF16),
            vm((2, 1, HD), F32), vm((2 * HD, D), BF16), vm((1, D), F32), vm((1, D), F32), vm((1, D), F32),
            vm((D, 6 * HD), BF16), vm((2, 2, 1, HD), F32), vm((2 * HD, D), BF16), vm((1, D), F32),
            vm((SPACE, HD), BF16),
            vm((NSEQ, SLAB, HD), BF16), vm((NSEQ, SLAB, HD), BF16),
            vm((5, ROWS, NSEQ * SLAB), BF16),
            vm((2, ROWS, HD), BF16), vm((ROWS, HD), BF16),
            vm((2, ROWS, 2 * HD), BF16), vm((ROWS, 2 * HD), BF16),
            vm((NY, ROWS, FEAT), BF16), vm((NY, ROWS, FEAT), BF16),
            vm((NY, ROWS, FEAT), BF16),
            vm((2, ROWS, HD), BF16),
            vm((NY, ROWS, FEAT), BF16), vm((NY, ROWS, FEAT), BF16),
            vm((ROWS, SLICE), BF16), vm((ROWS, SLICE), BF16),
            dma((15,)), dma((6,)), dma((6,)), dma((31,)), dma((31,)), dma((3,)), dma((3,)),
            dma((NY,)), dma((NY,)), dma((NY,)), dma((NY,)), dma((NY,)), dma((NY,)),
        ],
        compiler_params=pltpu.CompilerParams(
            collective_id=0, has_side_effects=True, vmem_limit_bytes=56 * 1024 * 1024
        ),
        name="spatial_temporal",
    )(
        tokens, spatial_query, spatial_key, spatial_value, spatial_gain, spatial_proj,
        spatial_gate.reshape(1, D), temporal_shift.reshape(1, D), temporal_scale.reshape(1, D),
        temporal_weights.transpose(1, 2, 0, 3).reshape(3, D, HD), temporal_gain, temporal_proj,
        temporal_gate.reshape(1, D),
    )
    return out.transpose(1, 0, 2)


def solution(mesh):
    placed = (
        P("seq", None, "tp"),
        P("seq", None, "tp"),
        P("seq", None, "tp"),
        P("seq", None, "tp"),
        P(None, "tp", None),
        P("tp", None),
        P(),
        P(),
        P(),
        P(None, "tp", None, None),
        P(None, "tp", None),
        P("tp", None),
        P(),
    )
    return jax.shard_map(
        local, mesh=mesh, in_specs=placed, out_specs=P(None, "seq", "tp"), check_vma=False
    )
```

```python
import functools

import jax
import jax.numpy as jnp
from jax import lax
from jax.experimental import pallas as pl
from jax.experimental.pallas import tpu as pltpu
from jax.sharding import PartitionSpec as P

NORM_EPS = 1e-06
MESH = pl.DeviceIdType.MESH
BF16 = jnp.bfloat16
F32 = jnp.float32

NX, NZ, NY = 4, 8, 8
NSEQ = NX * NZ
FRAMES = 32
SPACE = 192
PLACES = SPACE // NSEQ
HALF = PLACES // 2
HD = 128
D = 3072
ROWS = HALF * FRAMES
FEAT = D // NY
SLICE = FEAT // 2
SLAB = 16
SCALE = HD**-0.5


def head_norm(values, gain):
    square_mean = jnp.mean(values * values, axis=-1, keepdims=True)
    return (values * lax.rsqrt(square_mean + NORM_EPS) * gain).astype(BF16)


def dot(a, b):
    return jnp.dot(a, b, preferred_element_type=F32)


def dot_t(a, b):
    return lax.dot_general(a, b, (((1,), (1,)), ((), ())), preferred_element_type=F32)


def one_hot(targets, columns):
    rows = targets.shape[0]
    return jnp.where(
        lax.broadcasted_iota(jnp.int32, (rows, columns), 1) == targets, 1.0, 0.0
    ).astype(BF16)


def row_iota(rows):
    return lax.broadcasted_iota(jnp.int32, (rows, 1), 0)


def kernel(
    tok_h, q_h, k_h, v_h, sgain_h, proj_h, sgate_h, shift_h, scale_h, w_h, tgain_h, proj2_h, tgate_h,
    out_ref,
    tok, q, k, v, sgain, proj, sgate, shift, scale, w, tgain, proj2, tgate,
    heads, slab_out, slab_in, pick, hv, hs, tokbuf, toksend, part_out, part_in, mid, mod, th,
    part2_out, part2_in, osend, orecv,
    load_sem, wsend, wrecv, a_send, a_recv, x_send, x_recv, o_send, o_recv, e1s, e1r, e2s, e2r, e3s, e3r,
):
    s = lax.axis_index("seq")
    t = lax.axis_index("tp")
    y = t // 2
    c = t % 2
    xx = s // NZ
    z = s % NZ
    sib = (s, t + 1 - 2 * c)

    sigma = 1 - 2 * c

    def ydev(step):
        return (s, 2 * ((y + sigma * step + 2 * NY) % NY) + c)

    def seq_peer(dx, dz):
        return ((xx + dx) % NX) * NZ + (z + dz) % NZ

    hops = sorted(
        [(dx, dz) for dx in range(NX) for dz in range(NZ) if dx or dz],
        key=lambda d: -(min(d[0], NX - d[0]) + min(d[1], NZ - d[1])),
    )

    def remote(src, dst, ss, rs, device):
        return pltpu.make_async_remote_copy(
            src_ref=src, dst_ref=dst, send_sem=ss, recv_sem=rs, device_id=device, device_id_type=MESH
        )

    sent, arrived = [], set()

    def go(copy):
        copy.start()
        sent.append(copy)
        return copy

    def arrive(copy):
        copy.wait_recv()
        arrived.add(id(copy))

    own_cols = pl.multiple_of(c * (3 * HD), HD)
    rows_c = pl.multiple_of(c * HD, HD)
    loads = [
        (q_h.at[0], q), (k_h.at[0], k), (v_h.at[0], v), (sgain_h, sgain), (tok_h.at[0], tok),
        (proj_h, proj.at[pl.ds(rows_c, HD)]), (sgate_h, sgate),
        (scale_h, scale), (shift_h, shift), (tgain_h, tgain.at[c]),
        (w_h.at[0], w.at[:, pl.ds(own_cols, HD)]),
        (w_h.at[1], w.at[:, pl.ds(pl.multiple_of(own_cols + HD, HD), HD)]),
        (w_h.at[2], w.at[:, pl.ds(pl.multiple_of(own_cols + 2 * HD, HD), HD)]),
        (proj2_h, proj2.at[pl.ds(rows_c, HD)]), (tgate_h, tgate),
    ]
    loads = [pltpu.make_async_copy(a, b, load_sem.at[i]) for i, (a, b) in enumerate(loads)]
    for copy in loads:
        copy.start()

    barrier = pltpu.get_barrier_semaphore()
    for dx, dz in hops:
        pl.semaphore_signal(barrier, inc=1, device_id=(seq_peer(dx, dz), t), device_id_type=MESH)
    for step in range(1, NY):
        pl.semaphore_signal(barrier, inc=1, device_id=ydev(step), device_id_type=MESH)
    pl.semaphore_signal(barrier, inc=1, device_id=sib, device_id_type=MESH)

    for copy in loads[:4]:
        copy.wait()
    qn = head_norm(q[...].astype(F32), sgain[0])
    kn = head_norm(k[...].astype(F32), sgain[1])
    sc = dot_t(qn, kn) * SCALE
    ex = jnp.exp(sc - jnp.max(sc, axis=-1, keepdims=True))
    at = (ex / jnp.sum(ex, axis=-1, keepdims=True)).astype(BF16)
    heads[...] = dot(at, v[...]).astype(BF16)

    r = row_iota(NSEQ * SLAB)
    j, i = r // SLAB, r % SLAB
    loads[4].wait()
    tk = tok[...]
    col = lax.broadcasted_iota(jnp.int32, (SLICE, 2 * HD), 1)
    row = lax.broadcasted_iota(jnp.int32, (SLICE, 2 * HD), 0)
    rest = SLICE - HD
    spread = jnp.where(
        (row >= HD) & ((col == row - HD) | (col == row - HD + HD + rest)), 1.0, 0.0
    ).astype(BF16)
    tail = dot(tk, spread).astype(BF16)
    slab = dot(one_hot(jnp.where(i < PLACES, PLACES * j + i, -1), SPACE), heads[...])
    slab += dot(
        one_hot(jnp.where((i >= PLACES) & (i < 2 * PLACES), PLACES * j + i - PLACES, -1), SPACE), tk[:, :HD]
    )
    last = (i >= 2 * PLACES) & (i < 2 * PLACES + HALF)
    slab += dot(one_hot(jnp.where(last, PLACES * j + i - 2 * PLACES, -1), SPACE), tail[:, :HD])
    slab += dot(one_hot(jnp.where(last, PLACES * j + HALF + i - 2 * PLACES, -1), SPACE), tail[:, HD:])
    slab_out[...] = slab.astype(BF16).reshape(NSEQ, SLAB, HD)

    pl.semaphore_wait(barrier, len(hops) + NY)

    switch = [
        remote(slab_out.at[seq_peer(dx, dz)], slab_in.at[s], a_send.at[n], a_recv.at[n], (seq_peer(dx, dz), t))
        for n, (dx, dz) in enumerate(hops)
    ]
    for copy in switch:
        go(copy)
    slab_in[s] = slab_out[s]

    weights = [
        (proj_h, proj.at[pl.ds(rows_c, HD)]), (tgain_h, tgain.at[c]),
        (w_h.at[0], w.at[:, pl.ds(own_cols, HD)]),
        (w_h.at[1], w.at[:, pl.ds(pl.multiple_of(own_cols + HD, HD), HD)]),
        (w_h.at[2], w.at[:, pl.ds(pl.multiple_of(own_cols + 2 * HD, HD), HD)]),
        (proj2_h, proj2.at[pl.ds(rows_c, HD)]),
    ]
    weights = [remote(a, b, wsend.at[n], wrecv.at[n], sib) for n, (a, b) in enumerate(weights)]
    for copy in weights:
        go(copy)

    r = row_iota(ROWS)
    p, f = r // FRAMES, r % FRAMES
    pick[0] = one_hot(SLAB * f + HALF * c + p, NSEQ * SLAB)
    pick[1] = one_hot(SLAB * f + HALF * (1 - c) + p, NSEQ * SLAB)
    pick[2] = one_hot(SLAB * f + PLACES + HALF * c + p, NSEQ * SLAB)
    pick[3] = one_hot(SLAB * f + PLACES + HALF * (1 - c) + p, NSEQ * SLAB)
    pick[4] = one_hot(SLAB * f + 2 * PLACES + p, NSEQ * SLAB)

    for copy in switch:
        arrive(copy)
    got = slab_in[...].reshape(NSEQ * SLAB, HD)
    hs[...] = dot(pick[1], got).astype(BF16)
    lanes_c = pl.ds(rows_c, HD)
    swap_heads = remote(hs, hv.at[:, lanes_c], x_send.at[0], x_recv.at[0], sib)
    go(swap_heads)
    hv[:, lanes_c] = dot(pick[0], got).astype(BF16)
    toksend[:, :HD] = dot(pick[3], got).astype(BF16)
    third = dot(pick[4], got).astype(BF16)
    toksend[:, HD:] = third
    swap_tok = remote(toksend, tokbuf.at[c], x_send.at[1], x_recv.at[1], sib)
    go(swap_tok)
    tokbuf[c, :, :HD] = dot(pick[2], got).astype(BF16)
    tokbuf[c, :, HD:] = third

    def term(rows, weight, offset):
        place = (y - sigma * offset + 2 * NY) % NY
        return dot(rows, weight[:, pl.ds(pl.multiple_of(place * FEAT, HD), FEAT)])

    def post(bufs, n, slot, step):
        buf_out, buf_in, ss, rs = bufs
        return go(remote(buf_out.at[n, slot], buf_in.at[n, slot], ss.at[n, slot], rs.at[n, slot], ydev(step)))

    def fetch(bufs, n, slot, step):
        buf_out, buf_in, ss, rs = bufs
        arrive(remote(buf_out.at[n, slot], buf_in.at[n, slot], ss.at[n, slot], rs.at[n, slot], ydev(step)))
        return buf_in[n, slot].astype(F32)

    via = {4: -2, 3: -1, 5: 1, 1: -1, 7: 1, 2: -2, 6: 2}

    def reduce_start(bufs, rows, weight, chunks):
        for slot in (4, 3, 5, 1, 7):
            value = term(rows, weight, slot).astype(BF16)
            for at, n in enumerate(chunks):
                bufs[0][n, slot] = value[at * FRAMES : (at + 1) * FRAMES]
                post(bufs, n, slot, via[slot])
        return [term(rows, weight, slot) for slot in (2, 6, 0)]

    def reduce_forward(bufs, n, plus, minus):
        bufs[0][n, 2] = (plus + fetch(bufs, n, 4, -2) + fetch(bufs, n, 3, -1)).astype(BF16)
        post(bufs, n, 2, via[2])
        bufs[0][n, 6] = (minus + fetch(bufs, n, 5, 1)).astype(BF16)
        post(bufs, n, 6, via[6])

    def reduce_end(bufs, n, own):
        for slot in (1, 7, 2, 6):
            own = own + fetch(bufs, n, slot, via[slot])
        return own

    first = (part_out, part_in, e1s, e1r)
    second = (part2_out, part2_in, e3s, e3r)

    loads[5].wait()
    arrive(weights[0])
    arrive(swap_heads)
    waiting = reduce_start(first, hv[...], proj, range(HALF))

    arrive(swap_tok)
    lane = lax.broadcasted_iota(jnp.int32, (2 * HD, 1), 0)
    inner = lane - HD - rest * c
    base = jnp.where(lane < HD, lane, jnp.where((inner >= 0) & (inner < rest), HD + inner, -FEAT))
    own_tok = dot(tokbuf[0], one_hot(base, FEAT)) + dot(tokbuf[1], one_hot(base + SLICE, FEAT))
    loads[6].wait()
    cols_y = pl.ds(pl.multiple_of(y * FEAT, HD), FEAT)
    gate = sgate[:, cols_y]

    def rows_of(values, n):
        return values[n * FRAMES : (n + 1) * FRAMES]

    for n in range(HALF):
        reduce_forward(first, n, rows_of(waiting[0], n), rows_of(waiting[1], n))

    def pass_on(n, offset, slot, step):
        place = (y + sigma * offset + 2 * NY) % NY
        return go(remote(mid.at[n, place], mid.at[n, place], e2s.at[n, slot], e2r.at[n, slot], ydev(step)))

    def receive(n, offset):
        place = (y + sigma * offset + 2 * NY) % NY
        slot = offset % NY
        arrive(remote(mid.at[n, place], mid.at[n, place], e2s.at[n, slot], e2r.at[n, slot], ydev(1)))

    for n in range(HALF):
        total = reduce_end(first, n, rows_of(waiting[2], n))
        mid[n, y] = (rows_of(own_tok, n) + gate * total).astype(BF16)
        pass_on(n, 0, 6, 2)
        pass_on(n, 0, 2, -2)
        pass_on(n, 0, 7, 1)
        pass_on(n, 0, 1, -1)
    for n in range(HALF):
        receive(n, -2)
        pass_on(n, -2, 4, 2)
        pass_on(n, -2, 5, 1)
        receive(n, 2)
        pass_on(n, 2, 3, -1)

    for copy in loads[7:]:
        copy.wait()
    for copy in weights[1:]:
        arrive(copy)

    def temporal(n):
        sums = jnp.zeros((FRAMES, 1), F32)
        for b in range(NY):
            sums += jnp.sum(mid[n, b].astype(F32), axis=-1, keepdims=True)
        mean = sums * (1.0 / D)
        squares = jnp.zeros((FRAMES, 1), F32)
        for b in range(NY):
            centre = mid[n, b].astype(F32) - mean
            squares += jnp.sum(centre * centre, axis=-1, keepdims=True)
        inv = lax.rsqrt(squares * (1.0 / D) + NORM_EPS)
        for b in range(NY):
            cols = slice(b * FEAT, (b + 1) * FEAT)
            mod[:, cols] = (
                (mid[n, b].astype(F32) - mean) * inv * (1.0 + scale[:, cols]) + shift[:, cols]
            ).astype(BF16)
        acc = dot(mod[...], w[...])
        for h in range(2):
            part = acc[:, 3 * HD * h : 3 * HD * (h + 1)]
            qt = head_norm(part[:, :HD], tgain[h, 0])
            kt = head_norm(part[:, HD : 2 * HD], tgain[h, 1])
            vt = part[:, 2 * HD :].astype(BF16)
            st = dot_t(qt, kt) * SCALE
            et = jnp.exp(st - jnp.max(st, axis=-1, keepdims=True))
            att = (et / jnp.sum(et, axis=-1, keepdims=True)).astype(BF16)
            th[n, :, h * HD : (h + 1) * HD] = dot(att, vt).astype(BF16)

    waiting = []
    for n in range(HALF):
        for offset in (-1, 1, 3, -3, 4):
            receive(n, offset)
        temporal(n)
        waiting.append(reduce_start(second, th[n], proj2, [n]))
    for n in range(HALF):
        reduce_forward(second, n, waiting[n][0], waiting[n][1])
    gate = tgate[:, cols_y]
    feature = lax.broadcasted_iota(jnp.int32, (FEAT, SLICE), 0)
    column = lax.broadcasted_iota(jnp.int32, (FEAT, SLICE), 1)
    give = jnp.where(feature == column + SLICE * (1 - c), 1.0, 0.0).astype(BF16)
    keep = jnp.where(feature == column + SLICE * c, 1.0, 0.0).astype(BF16)
    swaps = []
    for n in range(HALF):
        total = reduce_end(second, n, waiting[n][2])
        out = (mid[n, y].astype(F32) + gate * total).astype(BF16)
        osend[n] = dot(out, give).astype(BF16)
        swaps.append(go(remote(osend.at[n], orecv.at[n], o_send.at[n], o_recv.at[n], sib)))
        out_ref[HALF * c + n] = dot(out, keep).astype(BF16)
    for n in range(HALF):
        arrive(swaps[n])
        out_ref[HALF * (1 - c) + n] = orecv[n]

    for copy in sent:
        copy.wait_send()


def local(
    tokens, spatial_query, spatial_key, spatial_value, spatial_gain, spatial_proj, spatial_gate,
    temporal_shift, temporal_scale, temporal_weights, temporal_gain, temporal_proj, temporal_gate,
):
    vm = pltpu.VMEM
    dma = pltpu.SemaphoreType.DMA
    blocks = vm((HALF, NY, FRAMES, FEAT), BF16)
    any_spec = pl.BlockSpec(memory_space=pltpu.HBM)
    out = pl.pallas_call(
        kernel,
        out_shape=jax.ShapeDtypeStruct((PLACES, FRAMES, SLICE), BF16),
        in_specs=[any_spec] * 13,
        out_specs=pl.BlockSpec(memory_space=pltpu.VMEM),
        scratch_shapes=[
            vm((SPACE, SLICE), BF16), vm((SPACE, HD), BF16), vm((SPACE, HD), BF16), vm((SPACE, HD), BF16),
            vm((2, 1, HD), F32), vm((2 * HD, D), BF16), vm((1, D), F32), vm((1, D), F32), vm((1, D), F32),
            vm((D, 6 * HD), BF16), vm((2, 2, 1, HD), F32), vm((2 * HD, D), BF16), vm((1, D), F32),
            vm((SPACE, HD), BF16),
            vm((NSEQ, SLAB, HD), BF16), vm((NSEQ, SLAB, HD), BF16),
            vm((5, ROWS, NSEQ * SLAB), BF16),
            vm((ROWS, 2 * HD), BF16), vm((ROWS, HD), BF16),
            vm((2, ROWS, 2 * HD), BF16), vm((ROWS, 2 * HD), BF16),
            blocks, blocks,
            blocks, vm((FRAMES, D), BF16),
            vm((HALF, FRAMES, 2 * HD), BF16),
            blocks, blocks,
            vm((HALF, FRAMES, SLICE), BF16), vm((HALF, FRAMES, SLICE), BF16),
            dma((15,)), dma((6,)), dma((6,)), dma((31,)), dma((31,)), dma((2,)), dma((2,)),
            dma((HALF,)), dma((HALF,)),
            dma((HALF, NY)), dma((HALF, NY)), dma((HALF, NY)), dma((HALF, NY)), dma((HALF, NY)), dma((HALF, NY)),
        ],
        compiler_params=pltpu.CompilerParams(
            collective_id=0, has_side_effects=True, vmem_limit_bytes=56 * 1024 * 1024
        ),
        name="spatial_temporal",
    )(
        tokens, spatial_query, spatial_key, spatial_value, spatial_gain, spatial_proj,
        spatial_gate.reshape(1, D), temporal_shift.reshape(1, D), temporal_scale.reshape(1, D),
        temporal_weights.transpose(1, 2, 0, 3).reshape(3, D, HD), temporal_gain, temporal_proj,
        temporal_gate.reshape(1, D),
    )
    return out.transpose(1, 0, 2)


def solution(mesh):
    placed = (
        P("seq", None, "tp"),
        P("seq", None, "tp"),
        P("seq", None, "tp"),
        P("seq", None, "tp"),
        P(None, "tp", None),
        P("tp", None),
        P(),
        P(),
        P(),
        P(None, "tp", None, None),
        P(None, "tp", None),
        P("tp", None),
        P(),
    )
    return jax.shard_map(
        local, mesh=mesh, in_specs=placed, out_specs=P(None, "seq", "tp"), check_vma=False
    )
```
